32 devices in a mesh: row: 8 (over y, x, core), col: 4 (over z).
Axes of the slice: x: 2, y: 2, z: 4, core: 2. Of those that a mesh axis runs over, the one named last changes fastest.
Arguments:
- x_blocks: bfloat16 [8, 4, 16, 128, 128], P('row', 'col'), may hold values from -0.8984375 to 0.8984375
- x_live: int32 [8, 4, 16], P('row', 'col'), may hold values 0 or 1
- pair_slots: int32 [8, 4, 4, 3, 192], P('row', 'col'), may hold values from 0 to 15
- pair_count: int32 [8, 4, 4], P('row', 'col'), may hold values from 15 to 192, as said below
Outputs:
- gram_blocks: float32 [8, 4, 16, 128, 128], P('row', 'col')
The draws below stay inside these ranges and needn't reach their ends.
Inputs may be any that keep to these rules, and one draw needn't show every extreme that they name: `pair_count`: live pairs of a tile at a section; some tile has exactly 192 at its first section.
All inputs are finite; a program needn't handle non-finite values. No bound on the sum of `x_live` on one device may be relied on, other than what follows from the above.
Results may differ from the reference program's by a relative error of at most 0.0003.
Values may be sent and summed in bfloat16 or wider, within the bound.
No kernel may reach another device: no remote copies, remote signals or barrier semaphores. Data moves between devices by JAX's collectives and lax.ppermute only.
A program may use at most 64 MiB of HBM per device.

```python
import jax
import jax.numpy as jnp
from jax import lax

BLK = 128
SLOTS = 16
PAIRS = 192
SECTIONS = 4
N_ROW = 8
N_COL = 4


def draw_pair_count(key, part):
    key_density, key_spread, key_busiest = jax.random.split(key, 3)
    density = jax.random.randint(key_density, (N_ROW, N_COL, 1), 1, 9)
    spread = jax.random.randint(key_spread, (N_ROW, N_COL, SECTIONS), 5, 9)
    busiest = jax.random.randint(key_busiest, (), 0, N_ROW * N_COL)
    tile_ids = lax.iota(jnp.int32, N_ROW * N_COL).reshape(N_ROW, N_COL, 1)
    density = jnp.where(tile_ids == busiest, 8, density)
    first_section = jnp.where(tile_ids[:, :, 0] == busiest, 8, spread[:, :, 0])
    spread = spread.at[:, :, 0].set(first_section)
    return (PAIRS * density * spread // 64).astype(jnp.int32)


def plant(entries, key, low, top_value):
    longest = entries.shape.index(max(entries.shape))
    spots = []
    for shift in (0, 1):
        where = [jax.random.randint(jax.random.fold_in(key, axis), (), 0, length) for axis, length in enumerate(entries.shape)]
        where[longest] = (where[longest] + shift) % entries.shape[longest]
        spots.append(tuple(where))
    return entries.at[spots[0]].set(low).at[spots[1]].set(top_value)


def level_of(key, dims, pieces, smallest, top_value):
    def one(dim, blocks):
        heights = jax.random.uniform(jax.random.fold_in(jax.random.fold_in(key, 6), dim), (blocks,), jnp.float32, smallest / len(pieces), top_value / len(pieces))
        return jnp.repeat(jnp.exp(heights), dims[dim] // blocks).reshape((-1,) + (1,) * (len(dims) - dim - 1))

    level = one(*pieces[0])
    for cut in pieces[1:]:
        level = level * one(*cut)
    return level


def centred(rng, extent, width, limit, cuts=(), held_as=jnp.bfloat16):
    gain = level_of(rng, extent, cuts, -0.22, 0.18) if cuts else 1.0
    entries = jax.random.normal(rng, extent, jnp.float32) * width * gain
    return jnp.minimum(jnp.maximum(entries, -limit), limit).astype(held_as)


def setup_inputs(seed: int = 0) -> dict:
    streams_of = jax.random.split(jax.random.key(seed), 5)
    x_blocks = centred(streams_of[0], (N_ROW, N_COL, SLOTS, BLK, BLK), 0.15, 0.8984375, ((0, 8), (1, 4)))
    x_live = plant((jax.random.randint(streams_of[1], (N_ROW, N_COL, SLOTS), 0, 4) < 3).astype(jnp.int32), jax.random.fold_in(streams_of[1], 1), 0, 1)
    pair_slots = plant(jax.random.randint(streams_of[2], (N_ROW, N_COL, SECTIONS, 3, PAIRS), 0, SLOTS), jax.random.fold_in(streams_of[2], 1), 0, SLOTS - 1).astype(jnp.int32)
    pair_count = draw_pair_count(jax.random.fold_in(streams_of[4], 71), 0)
    return dict(x_blocks=x_blocks, x_live=x_live, pair_slots=pair_slots, pair_count=pair_count)


def add_pairs(gram_sum, left_piece, right_piece, picked, live_pairs):
    block_size = 48

    def one_block(block_no, running):
        first_pair = block_no * block_size
        chosen = lax.dynamic_slice_in_dim(picked, first_pair, block_size, 1)
        positions = first_pair + lax.iota(jnp.int32, block_size)
        weights = (positions < live_pairs).astype(jnp.float32)
        left_rows = jnp.take(left_piece, chosen[0], axis=0).astype(jnp.float32)
        right_rows = jnp.take(right_piece, chosen[1], axis=0).astype(jnp.float32)
        product = jnp.einsum("pik,pjk->pij", left_rows, right_rows)
        return running.at[chosen[2]].add(product * weights[:, None, None])

    return lax.fori_loop(0, picked.shape[1] // block_size, one_block, gram_sum)


def reference(x_blocks, x_live, pair_slots, pair_count):
    layers = N_ROW // N_COL
    filtered = x_blocks * x_live.astype(x_blocks.dtype)[:, :, :, None, None]

    def one_tile(tile_id):
        row_here = tile_id // N_COL
        col_here = tile_id % N_COL
        panel_here = row_here // layers
        within = row_here % layers
        gram_sum = jnp.zeros((SLOTS, BLK, BLK), jnp.float32)
        for section_no in range(SECTIONS):
            left_piece = filtered[row_here, (col_here + section_no) % N_COL]
            right_piece = filtered[col_here * layers + within, (panel_here + section_no) % N_COL]
            gram_sum = add_pairs(gram_sum, left_piece, right_piece, pair_slots[row_here, col_here, section_no], pair_count[row_here, col_here, section_no])
        return gram_sum

    all_grams = lax.map(one_tile, jnp.arange(N_ROW * N_COL, dtype=jnp.int32))
    return all_grams.reshape(N_ROW, N_COL, SLOTS, BLK, BLK)
```

```python
import functools

import jax
import jax.numpy as jnp
from jax import lax
from jax.experimental import pallas as pl
from jax.experimental.pallas import tpu as pltpu
from jax.sharding import PartitionSpec as P

SECTIONS = 4
UNROLL = 26
AXES = ("row", "col")
ROWS_BY_ROWS = (((1,), (1,)), ((), ()))


def pair_codes(pair_slots, pair_count, slots):
    pairs = pair_slots.shape[2]
    place = lax.iota(jnp.int32, pairs)
    left, right, out = pair_slots[:, 0], pair_slots[:, 1], pair_slots[:, 2]
    live = place[None, :] < pair_count[:, None]
    same = (out[:, :, None] == out[:, None, :]) & live[:, :, None] & live[:, None, :]
    rank = jnp.sum((same & (place[None, :] < place[:, None])[None]).astype(jnp.int32), axis=2)
    slot_ids = lax.iota(jnp.int32, slots)
    held = jnp.sum(((out[:, :, None] == slot_ids) & live[:, :, None]).astype(jnp.int32), axis=1)
    entries = (held + 1) // 2
    before = (out[:, :, None] > slot_ids).astype(jnp.int32)
    entry = jnp.sum(before * entries[:, None, :], axis=2) + rank // 2
    first = rank % 2 == 0
    part = jnp.where(first, (left - slots) + right * 2**12 + out * 2**24, (left - slots) * 2**6 + right * 2**18)
    room = (pairs + slots) // 2
    room = (room + UNROLL - 1) // UNROLL * UNROLL
    here = (entry[:, None, :] == lax.iota(jnp.int32, room)[None, :, None]) & live[:, None, :]
    codes = slots + slots * 2**6 + jnp.sum(jnp.where(here, part[:, None, :], 0), axis=2)
    return codes, jnp.sum(entries, axis=1)


def product_kernel(cfg, codes, meta, *refs):
    t_first, tasks, lefts, rule, has_sum = cfg
    refs = list(refs)
    left_refs = [refs[2 * s : 2 * s + 2] for s in range(lefts)]
    refs = refs[2 * lefts :]
    right_refs = [refs[4 * i : 4 * i + 4] for i in range(tasks)]
    refs = refs[4 * tasks :]
    if has_sum:
        sum_ref = refs.pop(0)
    out, left_buf, right_buf, sems = refs
    slots = out.shape[0]
    half = slots // 2
    shift, near_x, near_y = meta[SECTIONS], meta[SECTIONS + 1], meta[SECTIONS + 2]

    def section_of(i):
        return lax.rem(t_first + i + shift, SECTIONS)

    def wanted(i):
        section = section_of(i)
        if rule == "early":
            return section < SECTIONS - 1
        if rule == "late":
            return (section == SECTIONS - 1) | (i == tasks - 1)
        return section >= 0

    def copies(i):
        section = section_of(i)
        wants = wanted(i)
        found = []
        for s in range(lefts):
            for h in range(2):
                to = left_buf.at[i, pl.ds(h * half, half)]
                found.append((wants & (section == s), pltpu.make_async_copy(left_refs[s][h], to, sems.at[i, h])))
        for h, near in ((0, near_y), (1, near_x)):
            to = right_buf.at[i, pl.ds(h * half, half)]
            for k in range(2):
                found.append(
                    (wants & (near == 1 - k), pltpu.make_async_copy(right_refs[i][2 * h + k], to, sems.at[i, 2 + h]))
                )
        return found

    for i in range(tasks):
        for condition, copy in copies(i):
            pl.when(condition)(copy.start)
    if has_sum:
        sum_copy = pltpu.make_async_copy(sum_ref, out, sems.at[tasks, 0])
        sum_copy.start()
    for i in range(tasks):
        left_buf[i, slots] = jnp.zeros(left_buf.shape[2:], left_buf.dtype)
    if has_sum:
        sum_copy.wait()
    else:
        out[...] = jnp.zeros_like(out)
    for i in range(tasks):
        for condition, copy in copies(i):
            pl.when(condition)(copy.wait)

    def one_task(i, carry):
        section = section_of(i)
        blocks = jnp.where(wanted(i), (meta[section] + UNROLL - 1) // UNROLL, 0)

        def one_block(block, carry):
            products = []
            for u in range(UNROLL):
                code = codes[section, block * UNROLL + u]
                left = [left_buf[i, (code >> k) & 63] for k in (0, 6)]
                right = [right_buf[i, (code >> k) & 63] for k in (12, 18)]
                products.append(
                    lax.dot_general(
                        jnp.concatenate(left, axis=1),
                        jnp.concatenate(right, axis=1),
                        ROWS_BY_ROWS,
                        preferred_element_type=jnp.float32,
                    )
                )
            for u in range(UNROLL):
                slot = codes[section, block * UNROLL + u] >> 24
                out[slot] += products[u]
            return carry

        return lax.fori_loop(0, blocks, one_block, carry)

    lax.fori_loop(0, tasks, one_task, 0)


def add_terms(codes, meta, left, right, running, t_first, rule, slots, side):
    tasks = len(right)
    operands = [codes, meta] + [h for pair in left for h in pair] + [h for four in right for h in four]
    if running is not None:
        operands.append(running)
    work = tasks * 96 * 2 * side * side * 2 * side
    return pl.pallas_call(
        functools.partial(product_kernel, (t_first, tasks, len(left), rule, running is not None)),
        out_shape=jax.ShapeDtypeStruct((slots, side, side), jnp.float32),
        in_specs=[pl.BlockSpec(memory_space=pltpu.SMEM)] * 2 + [pl.BlockSpec(memory_space=pl.ANY)] * (len(operands) - 2),
        out_specs=pl.BlockSpec(memory_space=pltpu.VMEM),
        scratch_shapes=[
            pltpu.VMEM((tasks, slots + 1, side, side), jnp.bfloat16),
            pltpu.VMEM((tasks, slots, side, side), jnp.bfloat16),
            pltpu.SemaphoreType.DMA((tasks + 1, 4)),
        ],
        compiler_params=pltpu.CompilerParams(vmem_limit_bytes=32 * 2**20),
        cost_estimate=pl.CostEstimate(flops=2 * work, bytes_accessed=4 * 2**20, transcendentals=0),
    )(*operands)


def body(x_blocks, x_live, pair_slots, pair_count):
    row_total = lax.axis_size("row")
    col_total = lax.axis_size("col")
    layers = row_total // col_total
    panel = lax.axis_index("row") // layers
    col = lax.axis_index("col")
    slots, side = x_blocks.shape[2], x_blocks.shape[3]
    half = slots // 2

    def place(p, w, z):
        return (p * layers + w) * col_total + z

    everyone = [(p, w, z) for p in range(col_total) for w in range(layers) for z in range(col_total)]

    def moved(value, source_of):
        pairs = []
        for p, w, z in everyone:
            q, y = source_of(p, z)
            pairs.append((place(q, w, y), place(p, w, z)))
        return lax.ppermute(value, AXES, pairs)

    live = x_live[0, 0].astype(jnp.bfloat16)[:, None, None]
    first = x_blocks[0, 0, :half] * live[:half], x_blocks[0, 0, half:] * live[half:]
    codes, entries = pair_codes(pair_slots[0, 0], pair_count[0, 0], slots)

    if col_total != SECTIONS:
        filtered = jnp.concatenate(first)
        left, right = [], []
        for s in range(SECTIONS):
            a = filtered if s == 0 else moved(filtered, lambda p, z: (p, (z + s) % col_total))
            b = moved(filtered, lambda p, z: (z, (p + s) % col_total))
            left.append((a[:half], a[half:]))
            right.append((b[:half], b[:half], b[half:], b[half:]))
        meta = jnp.concatenate([entries, jnp.zeros((4,), jnp.int32)])
        return add_terms(codes, meta, left, right, None, 0, "all", slots, side)[None, None]

    near_x = panel % 2 == col % 2
    near_y = panel // 2 == col // 2
    shift = (col - panel) % SECTIONS
    meta = jnp.concatenate([entries, jnp.stack([shift, near_x.astype(jnp.int32), near_y.astype(jnp.int32), 0 * shift])])

    left = [first]
    for s in range(1, SECTIONS):
        left.append(tuple(moved(h, lambda p, z: (p, (z + 1) % col_total)) for h in left[-1]))

    def spread(t):
        a, b = left[t]
        a = jnp.where(near_x, a, moved(a, lambda p, z: (p ^ 1, z)))
        b = jnp.where(near_y, b, moved(b, lambda p, z: (p ^ 2, z)))
        return a, moved(a, lambda p, z: (p ^ 2, z)), b, moved(b, lambda p, z: (p ^ 1, z))

    right = [spread(t) for t in range(SECTIONS)]
    total = add_terms(codes, meta, left[:3], right[:2], None, 0, "early", slots, side)
    total = add_terms(codes, meta, left, right[:3], total, 0, "late", slots, side)
    total = add_terms(codes, meta, left, right[3:], total, 3, "all", slots, side)
    return total[None, None]


def solution(mesh):
    return jax.shard_map(
        body,
        mesh=mesh,
        in_specs=(
            P("row", "col", None, None, None),
            P("row", "col", None),
            P("row", "col", None, None, None),
            P("row", "col", None),
        ),
        out_specs=P("row", "col", None, None, None),
        check_vma=False,
    )
```

```python
import functools

import jax
import jax.numpy as jnp
from jax import lax
from jax.experimental import pallas as pl
from jax.experimental.pallas import tpu as pltpu
from jax.sharding import PartitionSpec as P

SECTIONS = 4
UNROLL = 26
AXES = ("row", "col")
ROWS_BY_ROWS = (((1,), (1,)), ((), ()))
VLIM = 12
KSPACE = pl.ANY
AHEAD = True
KS = ({0: (0, 1), 1: (0, 1), 2: (0, 1)}, {0: (2, 3), 1: (2, 3), 2: (2, 3)}, {3: (0, 1, 2, 3)})
AFTER = {'L2B': ('Y0C', 'X0D'), 'X2A': ('X1A', 'Y1B'), 'Y2B': ('X1A', 'Y1B'), 'Y2A': ('Y1A', 'X1B'), 'X2B': ('Y1A', 'X1B'), 'L3B': ('R3A',)}


def pair_codes(pair_slots, pair_count, slots):
    pairs = pair_slots.shape[2]
    place = lax.iota(jnp.int32, pairs)
    left, right, out = pair_slots[:, 0], pair_slots[:, 1], pair_slots[:, 2]
    live = place[None, :] < pair_count[:, None]
    same = (out[:, :, None] == out[:, None, :]) & live[:, :, None] & live[:, None, :]
    rank = jnp.sum((same & (place[None, :] < place[:, None])[None]).astype(jnp.int32), axis=2)
    slot_ids = lax.iota(jnp.int32, slots)
    held = jnp.sum(((out[:, :, None] == slot_ids) & live[:, :, None]).astype(jnp.int32), axis=1)
    entries = (held + 1) // 2
    before = (out[:, :, None] > slot_ids).astype(jnp.int32)
    entry = jnp.sum(before * entries[:, None, :], axis=2) + rank // 2
    first = rank % 2 == 0
    part = jnp.where(first, (left - slots) + right * 2**12 + out * 2**24, (left - slots) * 2**6 + right * 2**18)
    room = (pairs + slots) // 2
    room = (room + UNROLL - 1) // UNROLL * UNROLL
    here = (entry[:, None, :] == lax.iota(jnp.int32, room)[None, :, None]) & live[:, None, :]
    codes = slots + slots * 2**6 + jnp.sum(jnp.where(here, part[:, None, :], 0), axis=2)
    return codes, jnp.sum(entries, axis=1)


def product_kernel(cfg, codes, meta, *refs):
    sections, allowed, tiles, left_of, right_of, has_sum = cfg
    tasks = len(sections)
    sum_ref = refs[-5] if has_sum else None
    out, left_buf, right_buf, sems = refs[-4:]
    slots = out.shape[0]
    shift = meta[SECTIONS]

    def tile_of(section):
        return lax.rem(section + SECTIONS - shift, SECTIONS)

    def wanted(i):
        tile = tile_of(sections[0] + i)
        yes = [tile == t for t in allowed[0]]
        if len(set(allowed)) > 1:
            yes = [(i == k) & (tile == t) for k in range(tasks) for t in allowed[k]]
        return functools.reduce(lambda a, b: a | b, yes)

    def copies(i):
        tile = tile_of(sections[i])
        wants = wanted(i)
        found = []
        start = 0
        for piece, (ref, size) in enumerate(left_of[i]):
            to = left_buf.at[i, pl.ds(start, size)]
            found.append((wants, pltpu.make_async_copy(refs[ref], to, sems.at[i, 0, piece])))
            start += size
        for t, pieces in zip(tiles, right_of):
            if t not in allowed[i]:
                continue
            start = 0
            for piece, (flag, near, far, size) in enumerate(pieces):
                to = right_buf.at[i, pl.ds(start, size)]
                sem = sems.at[i, 1, piece]
                if near == far:
                    found.append((tile == t, pltpu.make_async_copy(refs[near], to, sem)))
                else:
                    held = meta[SECTIONS + 1 + flag] == 1
                    found.append(((tile == t) & held, pltpu.make_async_copy(refs[near], to, sem)))
                    found.append(((tile == t) & ~held, pltpu.make_async_copy(refs[far], to, sem)))
                start += size
        return found

    for i in range(tasks):
        for condition, copy in copies(i):
            pl.when(condition)(copy.start)
    if has_sum:
        sum_copy = pltpu.make_async_copy(sum_ref, out, sems.at[tasks, 0, 0])
        sum_copy.start()
    for i in range(tasks):
        left_buf[i, slots] = jnp.zeros(left_buf.shape[2:], left_buf.dtype)
    if has_sum:
        sum_copy.wait()
    else:
        out[...] = jnp.zeros_like(out)
    for i in range(tasks):
        for condition, copy in copies(i):
            pl.when(condition)(copy.wait)

    def one_task(i, carry):
        section = sections[0] + i
        blocks = jnp.where(wanted(i), (meta[section] + UNROLL - 1) // UNROLL, 0)

        def one_block(block, carry):
            products = []
            for u in range(UNROLL):
                code = codes[section, block * UNROLL + u]
                left = [left_buf[i, (code >> k) & 63] for k in (0, 6)]
                right = [right_buf[i, (code >> k) & 63] for k in (12, 18)]
                products.append(
                    lax.dot_general(
                        jnp.concatenate(left, axis=1),
                        jnp.concatenate(right, axis=1),
                        ROWS_BY_ROWS,
                        preferred_element_type=jnp.float32,
                    )
                )
            for u in range(UNROLL):
                slot = codes[section, block * UNROLL + u] >> 24
                out[slot] += products[u]
            return carry

        return lax.fori_loop(0, blocks, one_block, carry)

    lax.fori_loop(0, tasks, one_task, 0)


def add_terms(codes, meta, left, right, running, stage, slots, side):
    sections, allowed = tuple(stage), tuple(stage.values())
    tiles = tuple(sorted({t for some in allowed for t in some}))
    tasks = len(sections)
    operands = []

    def place(value):
        for k, known in enumerate(operands):
            if known is value:
                return k
        operands.append(value)
        return len(operands) - 1

    left_of = tuple(tuple((place(v), v.shape[0]) for v in left[s]) for s in sections)
    right_of = tuple(tuple((f, place(u), place(v), u.shape[0]) for f, u, v in right[t]) for t in tiles)
    if running is not None:
        operands.append(running)
    work = tasks * 96 * 2 * side * side * 2 * side
    return pl.pallas_call(
        functools.partial(product_kernel, (sections, allowed, tiles, left_of, right_of, running is not None)),
        out_shape=jax.ShapeDtypeStruct((slots, side, side), jnp.float32),
        in_specs=[pl.BlockSpec(memory_space=pltpu.SMEM)] * 2 + [pl.BlockSpec(memory_space=KSPACE)] * len(operands),
        out_specs=pl.BlockSpec(memory_space=pltpu.VMEM),
        scratch_shapes=[
            pltpu.VMEM((tasks, slots + 1, side, side), jnp.bfloat16),
            pltpu.VMEM((tasks, slots, side, side), jnp.bfloat16),
            pltpu.SemaphoreType.DMA((tasks + 1, 2, 2)),
        ],
        compiler_params=pltpu.CompilerParams(vmem_limit_bytes=VLIM * 2**20),
        cost_estimate=pl.CostEstimate(flops=2 * work, bytes_accessed=4 * 2**20, transcendentals=0),
    )(codes, meta, *operands)


def body(x_blocks, x_live, pair_slots, pair_count):
    row_total = lax.axis_size("row")
    col_total = lax.axis_size("col")
    layers = row_total // col_total
    panel = lax.axis_index("row") // layers
    col = lax.axis_index("col")
    slots, side = x_blocks.shape[2], x_blocks.shape[3]
    half = slots // 2

    def place(p, w, z):
        return (p * layers + w) * col_total + z

    everyone = [(p, w, z) for p in range(col_total) for w in range(layers) for z in range(col_total)]

    def moved(value, source_of):
        pairs = []
        for p, w, z in everyone:
            if source_of(p, z) is not None:
                q, y = source_of(p, z)
                pairs.append((place(q, w, y), place(p, w, z)))
        return lax.ppermute(value, AXES, pairs)

    filtered = jnp.where(x_live[0, 0][:, None, None] != 0, x_blocks[0, 0], jnp.zeros((), x_blocks.dtype))
    codes, entries = pair_codes(pair_slots[0, 0], pair_count[0, 0], slots)

    if col_total != SECTIONS:
        left, right = [], []
        for s in range(SECTIONS):
            left.append([filtered if s == 0 else moved(filtered, lambda p, z: (p, (z + s) % col_total))])
            value = moved(filtered, lambda p, z: (z, (p + s) % col_total))
            right.append([(0, value, value)])
        meta = jnp.concatenate([entries, jnp.zeros((4,), jnp.int32)])
        everything = {s: tuple(range(SECTIONS)) for s in range(SECTIONS)}
        total = add_terms(codes, meta, left, right, None, everything, slots, side)
        return total[None, None]

    near_x = panel % 2 == col % 2
    near_y = panel // 2 == col // 2
    next_y = panel // 2 == (col + 1) % SECTIONS // 2
    shift = (col - panel) % SECTIONS
    meta = jnp.concatenate([entries, jnp.stack([shift, near_x.astype(jnp.int32), near_y.astype(jnp.int32), 0 * shift])])
    done = {}

    def hop(name, value, source_of):
        waits = AFTER.get(name, ())
        if waits:
            value = lax.optimization_barrier((value,) + tuple(done[n] for n in waits))[0]
        with jax.named_scope(name):
            done[name] = moved(value, source_of)
        return done[name]

    def in_plane(name, value, flip, offset, far=False):
        def source_of(p, z):
            q = (z + offset) % SECTIONS
            return (p ^ flip, z) if p ^ flip == q or (far and p ^ flip == q ^ (3 - flip)) else None

        return hop(name, value, source_of)

    def along(name, value, by):
        return hop(name, value, lambda p, z: (p, (z + by) % SECTIONS))

    near = {1: near_x, 2: near_y}

    def stage_kernel(name, before, stage):
        done[name] = add_terms(codes, meta, left, right, done.get(before), stage, slots, side)

    made = {"a0": filtered[:half], "b0": filtered[half:]}
    ops = {}

    def op(name, operand, source_of):
        ops[name] = (operand, source_of)

    def get(name):
        if name not in made:
            if name in ops:
                operand, source_of = ops[name]
                value = operand()
                waits = [get(w) for w in AFTER.get(name, ())]
                if waits:
                    value = lax.optimization_barrier((value, *waits))[0]
                made[name] = moved(value, source_of)
            else:
                made[name] = values[name]()
        return made[name]

    def x_hop(p, z):
        return p ^ 1, z

    def y_hop(p, z):
        return p ^ 2, z

    def next_col(p, z):
        return p, (z + 1) % SECTIONS

    def last_col(p, z):
        return p, (z - 1) % SECTIONS

    values = {}
    for t in range(SECTIONS):
        la, lb = ("a0", "b0") if t == 0 else (f"L{t}A", f"L{t}B")
        if t:
            pa, pb = ("a0", "b0") if t == 1 else (f"L{t - 1}A", f"L{t - 1}B")
            op(la, functools.partial(get, pa), next_col)
            op(lb, functools.partial(get, pb), next_col)
        if t < SECTIONS - 1 or not AHEAD:
            op(f"X{t}A", functools.partial(get, la), x_hop)
            op(f"Y{t}B", functools.partial(get, lb), y_hop)
            values[f"S{t}A"] = lambda t=t, la=la: jnp.where(near_x, get(la), get(f"X{t}A"))
            values[f"S{t}B"] = lambda t=t, lb=lb: jnp.where(near_y, get(lb), get(f"Y{t}B"))
            op(f"Y{t}A", functools.partial(get, f"S{t}A"), y_hop)
            op(f"X{t}B", functools.partial(get, f"S{t}B"), x_hop)
    if AHEAD:
        values["S0C"] = lambda: jnp.where(near_x, get("X0A"), get("a0"))
        values["S0D"] = lambda: jnp.where(next_y, get("b0"), get("Y0B"))
        op("Y0C", functools.partial(get, "S0C"), y_hop)
        op("X0D", functools.partial(get, "S0D"), x_hop)
        values["F0C"] = lambda: jnp.where(next_y, get("S0C"), get("Y0C"))
        values["F0D"] = lambda: jnp.where(near_x, get("X0D"), get("S0D"))
        op("R3A", functools.partial(get, "F0C"), last_col)
        op("R3B", functools.partial(get, "F0D"), last_col)

    def left_of(s):
        return [get("a0"), get("b0")] if s == 0 else [get(f"L{s}A"), get(f"L{s}B")]

    def right_of(t):
        if AHEAD and t == SECTIONS - 1:
            return [(0, get("R3A"), get("R3A")), (0, get("R3B"), get("R3B"))]
        return [(1, get(f"S{t}A"), get(f"Y{t}A")), (0, get(f"S{t}B"), get(f"X{t}B"))]

    def kernel_stage(k):
        stage = KS[k]
        tiles = sorted({t for some in stage.values() for t in some})
        left, right = {s: left_of(s) for s in stage}, {t: right_of(t) for t in tiles}
        running = get(f"K{k - 1}") if k else None
        waits = [get(w) for w in AFTER.get(f"K{k}", ())]
        c = codes
        if waits:
            c = lax.optimization_barrier((codes, *waits))[0]
        return add_terms(c, meta, left, right, running, stage, slots, side)

    for k in range(len(KS)):
        values[f"K{k}"] = functools.partial(kernel_stage, k)
    done["K3"] = get(f"K{len(KS) - 1}")
    return done["K3"][None, None]


def solution(mesh):
    return jax.shard_map(
        body,
        mesh=mesh,
        in_specs=(
            P("row", "col", None, None, None),
            P("row", "col", None),
            P("row", "col", None, None, None),
            P("row", "col", None),
        ),
        out_specs=P("row", "col", None, None, None),
        check_vma=False,
    )
```

```python
import functools

import jax
import jax.numpy as jnp
from jax import lax
from jax.experimental import pallas as pl
from jax.experimental.pallas import tpu as pltpu
from jax.sharding import PartitionSpec as P

SECTIONS = 4
UNROLL = 26
AXES = ("row", "col")
ROWS_BY_ROWS = (((1,), (1,)), ((), ()))
VLIM = 12
KSPACE = pl.ANY
AHEAD = 'AB'
FIRST = 8
COST = 0.25
KS = ({0: (0, 1), 1: (0, 1), 2: (0, 1)}, {0: (2, 3), 1: (2, 3), 2: (2, 3)}, {3: (0, 1, 2, 3)})
AFTER = {'L2B': ('Y0C',), 'L3A': ('R3B',), 'L3B': ('R3A',), 'X2A': ('X1A', 'Y1B'), 'X2B': ('X1A', 'X1B', 'Y1A', 'Y1B'), 'Y0C': ('X0A',), 'Y2A': ('X1A', 'Y1A', 'Y1B'), 'Y2B': ('X1A', 'Y1B')}


def pair_codes(pair_slots, pair_count, slots):
    pairs = pair_slots.shape[2]
    place = lax.iota(jnp.int32, pairs)
    left, right, out = pair_slots[:, 0], pair_slots[:, 1], pair_slots[:, 2]
    live = place[None, :] < pair_count[:, None]
    same = (out[:, :, None] == out[:, None, :]) & live[:, :, None] & live[:, None, :]
    rank = jnp.sum((same & (place[None, :] < place[:, None])[None]).astype(jnp.int32), axis=2)
    slot_ids = lax.iota(jnp.int32, slots)
    held = jnp.sum(((out[:, :, None] == slot_ids) & live[:, :, None]).astype(jnp.int32), axis=1)
    entries = (held + 1) // 2
    before = (out[:, :, None] > slot_ids).astype(jnp.int32)
    entry = jnp.sum(before * entries[:, None, :], axis=2) + rank // 2
    first = rank % 2 == 0
    part = jnp.where(first, (left - slots) + right * 2**12 + out * 2**24, (left - slots) * 2**6 + right * 2**18)
    room = (pairs + slots) // 2
    room = (room + UNROLL - 1) // UNROLL * UNROLL
    here = (entry[:, None, :] == lax.iota(jnp.int32, room)[None, :, None]) & live[:, None, :]
    codes = slots + slots * 2**6 + jnp.sum(jnp.where(here, part[:, None, :], 0), axis=2)
    return codes, jnp.sum(entries, axis=1)


def product_kernel(cfg, codes, meta, *refs):
    sections, allowed, tiles, left_of, right_of, has_sum = cfg
    tasks = len(sections)
    sum_ref = refs[-5] if has_sum else None
    out, left_buf, right_buf, sems = refs[-4:]
    slots = out.shape[0]
    shift = meta[SECTIONS]

    def tile_of(section):
        return lax.rem(section + SECTIONS - shift, SECTIONS)

    def wanted(i):
        tile = tile_of(sections[0] + i)
        yes = [tile == t for t in allowed[0]]
        if len(set(allowed)) > 1:
            yes = [(i == k) & (tile == t) for k in range(tasks) for t in allowed[k]]
        return functools.reduce(lambda a, b: a | b, yes)

    def copies(i):
        tile = tile_of(sections[i])
        wants = wanted(i)
        found = []
        start = 0
        for piece, (ref, size) in enumerate(left_of[i]):
            to = left_buf.at[i, pl.ds(start, size)]
            found.append((wants, pltpu.make_async_copy(refs[ref], to, sems.at[i, 0, piece])))
            start += size
        for t, pieces in zip(tiles, right_of):
            if t not in allowed[i]:
                continue
            start = 0
            for piece, (flag, near, far, size) in enumerate(pieces):
                to = right_buf.at[i, pl.ds(start, size)]
                sem = sems.at[i, 1, piece]
                if near == far:
                    found.append((tile == t, pltpu.make_async_copy(refs[near], to, sem)))
                else:
                    held = meta[SECTIONS + 1 + flag] == 1
                    found.append(((tile == t) & held, pltpu.make_async_copy(refs[near], to, sem)))
                    found.append(((tile == t) & ~held, pltpu.make_async_copy(refs[far], to, sem)))
                start += size
        return found

    for i in range(tasks):
        for condition, copy in copies(i):
            pl.when(condition)(copy.start)
    if has_sum:
        sum_copy = pltpu.make_async_copy(sum_ref, out, sems.at[tasks, 0, 0])
        sum_copy.start()
    for i in range(tasks):
        left_buf[i, slots] = jnp.zeros(left_buf.shape[2:], left_buf.dtype)
    if not has_sum:
        out[...] = jnp.zeros_like(out)

    def arrived(i):
        for side, (buf, sizes) in enumerate(
            ((left_buf, [n for _, n in left_of[0]]), (right_buf, [n for *_, n in right_of[0]]))
        ):
            start = 0
            for piece, size in enumerate(sizes):
                there = buf.at[i, pl.ds(start, size)]
                pltpu.make_async_copy(there, there, sems.at[i, side, piece]).wait()
                start += size

    if has_sum:
        sum_copy.wait()

    def one_task(i, carry):
        section = sections[0] + i
        pl.when(wanted(i))(lambda: arrived(i))
        blocks = jnp.where(wanted(i), (meta[section] + UNROLL - 1) // UNROLL, 0)

        def one_block(block, carry):
            products = []
            for u in range(UNROLL):
                code = codes[section, block * UNROLL + u]
                left = [left_buf[i, (code >> k) & 63] for k in (0, 6)]
                right = [right_buf[i, (code >> k) & 63] for k in (12, 18)]
                products.append(
                    lax.dot_general(
                        jnp.concatenate(left, axis=1),
                        jnp.concatenate(right, axis=1),
                        ROWS_BY_ROWS,
                        preferred_element_type=jnp.float32,
                    )
                )
            for u in range(UNROLL):
                slot = codes[section, block * UNROLL + u] >> 24
                out[slot] += products[u]
            return carry

        return lax.fori_loop(0, blocks, one_block, carry)

    lax.fori_loop(0, tasks, one_task, 0)


def add_terms(codes, meta, left, right, running, stage, slots, side):
    sections, allowed = tuple(stage), tuple(stage.values())
    tiles = tuple(sorted({t for some in allowed for t in some}))
    tasks = len(sections)
    operands = []

    def place(value):
        for k, known in enumerate(operands):
            if known is value:
                return k
        operands.append(value)
        return len(operands) - 1

    left_of = tuple(tuple((place(v), v.shape[0]) for v in left[s]) for s in sections)
    right_of = tuple(tuple((f, place(u), place(v), u.shape[0]) for f, u, v in right[t]) for t in tiles)
    if running is not None:
        operands.append(running)
    work = tasks * 96 * 2 * side * side * 2 * side
    return pl.pallas_call(
        functools.partial(product_kernel, (sections, allowed, tiles, left_of, right_of, running is not None)),
        out_shape=jax.ShapeDtypeStruct((slots, side, side), jnp.float32),
        in_specs=[pl.BlockSpec(memory_space=pltpu.SMEM)] * 2 + [pl.BlockSpec(memory_space=KSPACE)] * len(operands),
        out_specs=pl.BlockSpec(memory_space=pltpu.VMEM),
        scratch_shapes=[
            pltpu.VMEM((tasks, slots + 1, side, side), jnp.bfloat16),
            pltpu.VMEM((tasks, slots, side, side), jnp.bfloat16),
            pltpu.SemaphoreType.DMA((tasks + 1, 2, 2)),
        ],
        compiler_params=pltpu.CompilerParams(vmem_limit_bytes=VLIM * 2**20),
        cost_estimate=pl.CostEstimate(flops=int(COST * work), bytes_accessed=4 * 2**20, transcendentals=0),
    )(codes, meta, *operands)


def body(x_blocks, x_live, pair_slots, pair_count):
    row_total = lax.axis_size("row")
    col_total = lax.axis_size("col")
    layers = row_total // col_total
    panel = lax.axis_index("row") // layers
    col = lax.axis_index("col")
    slots, side = x_blocks.shape[2], x_blocks.shape[3]
    half = slots // 2

    def place(p, w, z):
        return (p * layers + w) * col_total + z

    everyone = [(p, w, z) for p in range(col_total) for w in range(layers) for z in range(col_total)]

    def moved(value, source_of):
        pairs = []
        for p, w, z in everyone:
            if source_of(p, z) is not None:
                q, y = source_of(p, z)
                pairs.append((place(q, w, y), place(p, w, z)))
        return lax.ppermute(value, AXES, pairs)

    filtered = jnp.where(x_live[0, 0][:, None, None] != 0, x_blocks[0, 0], jnp.zeros((), x_blocks.dtype))
    codes, entries = pair_codes(pair_slots[0, 0], pair_count[0, 0], slots)

    if col_total != SECTIONS:
        left, right = [], []
        for s in range(SECTIONS):
            left.append([filtered if s == 0 else moved(filtered, lambda p, z: (p, (z + s) % col_total))])
            value = moved(filtered, lambda p, z: (z, (p + s) % col_total))
            right.append([(0, value, value)])
        meta = jnp.concatenate([entries, jnp.zeros((4,), jnp.int32)])
        everything = {s: tuple(range(SECTIONS)) for s in range(SECTIONS)}
        total = add_terms(codes, meta, left, right, None, everything, slots, side)
        return total[None, None]

    near_x = panel % 2 == col % 2
    near_y = panel // 2 == col // 2
    next_y = panel // 2 == (col + 1) % SECTIONS // 2
    shift = (col - panel) % SECTIONS
    meta = jnp.concatenate([entries, jnp.stack([shift, near_x.astype(jnp.int32), near_y.astype(jnp.int32), 0 * shift])])
    done = {}

    def hop(name, value, source_of):
        waits = AFTER.get(name, ())
        if waits:
            value = lax.optimization_barrier((value,) + tuple(done[n] for n in waits))[0]
        with jax.named_scope(name):
            done[name] = moved(value, source_of)
        return done[name]

    def in_plane(name, value, flip, offset, far=False):
        def source_of(p, z):
            q = (z + offset) % SECTIONS
            return (p ^ flip, z) if p ^ flip == q or (far and p ^ flip == q ^ (3 - flip)) else None

        return hop(name, value, source_of)

    def along(name, value, by):
        return hop(name, value, lambda p, z: (p, (z + by) % SECTIONS))

    near = {1: near_x, 2: near_y}

    def stage_kernel(name, before, stage):
        done[name] = add_terms(codes, meta, left, right, done.get(before), stage, slots, side)

    made = {"a0": filtered[:FIRST], "b0": filtered[FIRST:]}
    ops = {}

    def op(name, operand, source_of):
        ops[name] = (operand, source_of)

    def get(name):
        if name not in made:
            if name in ops:
                operand, source_of = ops[name]
                value = operand()
                waits = [get(w) for w in AFTER.get(name, ())]
                if waits:
                    value = lax.optimization_barrier((value, *waits))[0]
                with jax.named_scope(name):
                    made[name] = moved(value, source_of)
            else:
                made[name] = values[name]()
        return made[name]

    def x_hop(p, z):
        return p ^ 1, z

    def y_hop(p, z):
        return p ^ 2, z

    def next_col(p, z):
        return p, (z + 1) % SECTIONS

    def last_col(p, z):
        return p, (z - 1) % SECTIONS

    values = {}
    for t in range(SECTIONS):
        la, lb = ("a0", "b0") if t == 0 else (f"L{t}A", f"L{t}B")
        if t:
            pa, pb = ("a0", "b0") if t == 1 else (f"L{t - 1}A", f"L{t - 1}B")
            op(la, functools.partial(get, pa), next_col)
            op(lb, functools.partial(get, pb), next_col)
        if t < SECTIONS - 1 or "A" not in AHEAD:
            op(f"X{t}A", functools.partial(get, la), x_hop)
            values[f"S{t}A"] = lambda t=t, la=la: lax.select(near_x, get(la), get(f"X{t}A"))
            op(f"Y{t}A", functools.partial(get, f"S{t}A"), y_hop)
        if t < SECTIONS - 1 or "B" not in AHEAD:
            op(f"Y{t}B", functools.partial(get, lb), y_hop)
            values[f"S{t}B"] = lambda t=t, lb=lb: lax.select(near_y, get(lb), get(f"Y{t}B"))
            op(f"X{t}B", functools.partial(get, f"S{t}B"), x_hop)
    if AHEAD:
        values["S0C"] = lambda: lax.select(near_x, get("X0A"), get("a0"))
        values["S0D"] = lambda: lax.select(next_y, get("b0"), get("Y0B"))
        op("Y0C", functools.partial(get, "S0C"), y_hop)
        op("X0D", functools.partial(get, "S0D"), x_hop)
        values["F0C"] = lambda: lax.select(next_y, get("S0C"), get("Y0C"))
        values["F0D"] = lambda: lax.select(near_x, get("X0D"), get("S0D"))
        op("R3A", functools.partial(get, "F0C"), last_col)
        op("R3B", functools.partial(get, "F0D"), last_col)

    def left_of(s):
        return [get("a0"), get("b0")] if s == 0 else [get(f"L{s}A"), get(f"L{s}B")]

    def right_of(t):
        ahead = AHEAD if t == SECTIONS - 1 else ""
        a = (0, get("R3A"), get("R3A")) if "A" in ahead else (1, get(f"S{t}A"), get(f"Y{t}A"))
        b = (0, get("R3B"), get("R3B")) if "B" in ahead else (0, get(f"S{t}B"), get(f"X{t}B"))
        return [a, b]

    def kernel_stage(k):
        stage = KS[k]
        tiles = sorted({t for some in stage.values() for t in some})
        left, right = {s: left_of(s) for s in stage}, {t: right_of(t) for t in tiles}
        running = get(f"K{k - 1}") if k else None
        waits = [get(w) for w in AFTER.get(f"K{k}", ())]
        c = codes
        if waits:
            c = lax.optimization_barrier((codes, *waits))[0]
        return add_terms(c, meta, left, right, running, stage, slots, side)

    for k in range(len(KS)):
        values[f"K{k}"] = functools.partial(kernel_stage, k)
    done["K3"] = get(f"K{len(KS) - 1}")
    return done["K3"][None, None]


def solution(mesh):
    return jax.shard_map(
        body,
        mesh=mesh,
        in_specs=(
            P("row", "col", None, None, None),
            P("row", "col", None),
            P("row", "col", None, None, None),
            P("row", "col", None),
        ),
        out_specs=P("row", "col", None, None, None),
        check_vma=False,
    )
```

```python
import functools

import jax
import jax.numpy as jnp
from jax import lax
from jax.experimental import pallas as pl
from jax.experimental.pallas import tpu as pltpu
from jax.sharding import PartitionSpec as P

SECTIONS = 4
UNROLL = 26
AXES = ("row", "col")
ROWS_BY_ROWS = (((1,), (1,)), ((), ()))

STAGES = (
    {0: (0, 1), 1: (0, 1), 2: (0, 1)},
    {0: (2, 3), 1: (2, 3), 2: (2, 3)},
    {3: (0, 1, 2, 3)},
)

AFTER = {
    "L2B": ("Y0C",),
    "L3A": ("R3B",),
    "L3B": ("R3A",),
    "X2A": ("X1A", "Y1B"),
    "X2B": ("X1A", "X1B", "Y1A", "Y1B"),
    "Y0C": ("X0A",),
    "Y2A": ("X1A", "Y1A", "Y1B"),
    "Y2B": ("X1A", "Y1B"),
}


def pair_codes(pair_slots, pair_count, slots):
    pairs = pair_slots.shape[2]
    place = lax.iota(jnp.int32, pairs)
    left, right, out = pair_slots[:, 0], pair_slots[:, 1], pair_slots[:, 2]
    live = place[None, :] < pair_count[:, None]
    same = (out[:, :, None] == out[:, None, :]) & live[:, :, None] & live[:, None, :]
    rank = jnp.sum((same & (place[None, :] < place[:, None])[None]).astype(jnp.int32), axis=2)
    slot_ids = lax.iota(jnp.int32, slots)
    held = jnp.sum(((out[:, :, None] == slot_ids) & live[:, :, None]).astype(jnp.int32), axis=1)
    entries = (held + 1) // 2
    before = (out[:, :, None] > slot_ids).astype(jnp.int32)
    entry = jnp.sum(before * entries[:, None, :], axis=2) + rank // 2
    first = rank % 2 == 0
    part = jnp.where(first, (left - slots) + right * 2**12 + out * 2**24, (left - slots) * 2**6 + right * 2**18)
    room = (pairs + slots) // 2
    room = (room + UNROLL - 1) // UNROLL * UNROLL
    here = (entry[:, None, :] == lax.iota(jnp.int32, room)[None, :, None]) & live[:, None, :]
    codes = slots + slots * 2**6 + jnp.sum(jnp.where(here, part[:, None, :], 0), axis=2)
    return codes, jnp.sum(entries, axis=1)


def product_kernel(cfg, codes, meta, *refs):
    sections, allowed, tiles, left_of, right_of, has_sum = cfg
    tasks = len(sections)
    sum_ref = refs[-5] if has_sum else None
    out, left_buf, right_buf, sems = refs[-4:]
    slots = out.shape[0]
    shift = meta[SECTIONS]

    def tile_of(section):
        return lax.rem(section + SECTIONS - shift, SECTIONS)

    def wanted(i):
        tile = tile_of(sections[0] + i)
        yes = [tile == t for t in allowed[0]]
        if len(set(allowed)) > 1:
            yes = [(i == k) & (tile == t) for k in range(tasks) for t in allowed[k]]
        return functools.reduce(lambda a, b: a | b, yes)

    def copies(i):
        tile = tile_of(sections[i])
        wants = wanted(i)
        found = []
        start = 0
        for piece, (ref, size) in enumerate(left_of[i]):
            to = left_buf.at[i, pl.ds(start, size)]
            found.append((wants, pltpu.make_async_copy(refs[ref], to, sems.at[i, 0, piece])))
            start += size
        for t, pieces in zip(tiles, right_of):
            if t not in allowed[i]:
                continue
            start = 0
            for piece, (flag, near, far, size) in enumerate(pieces):
                to = right_buf.at[i, pl.ds(start, size)]
                sem = sems.at[i, 1, piece]
                if near == far:
                    found.append((tile == t, pltpu.make_async_copy(refs[near], to, sem)))
                else:
                    held = meta[SECTIONS + 1 + flag] == 1
                    found.append(((tile == t) & held, pltpu.make_async_copy(refs[near], to, sem)))
                    found.append(((tile == t) & ~held, pltpu.make_async_copy(refs[far], to, sem)))
                start += size
        return found

    for i in range(tasks):
        for condition, copy in copies(i):
            pl.when(condition)(copy.start)
    if has_sum:
        sum_copy = pltpu.make_async_copy(sum_ref, out, sems.at[tasks, 0, 0])
        sum_copy.start()
    for i in range(tasks):
        left_buf[i, slots] = jnp.zeros(left_buf.shape[2:], left_buf.dtype)
    if not has_sum:
        out[...] = jnp.zeros_like(out)

    def arrived(i):
        for side, (buf, sizes) in enumerate(
            ((left_buf, [n for _, n in left_of[0]]), (right_buf, [n for *_, n in right_of[0]]))
        ):
            start = 0
            for piece, size in enumerate(sizes):
                there = buf.at[i, pl.ds(start, size)]
                pltpu.make_async_copy(there, there, sems.at[i, side, piece]).wait()
                start += size

    if has_sum:
        sum_copy.wait()

    def one_task(i, carry):
        section = sections[0] + i
        pl.when(wanted(i))(lambda: arrived(i))
        blocks = jnp.where(wanted(i), (meta[section] + UNROLL - 1) // UNROLL, 0)

        def one_block(block, carry):
            products = []
            for u in range(UNROLL):
                code = codes[section, block * UNROLL + u]
                left = [left_buf[i, (code >> k) & 63] for k in (0, 6)]
                right = [right_buf[i, (code >> k) & 63] for k in (12, 18)]
                products.append(
                    lax.dot_general(
                        jnp.concatenate(left, axis=1),
                        jnp.concatenate(right, axis=1),
                        ROWS_BY_ROWS,
                        preferred_element_type=jnp.float32,
                    )
                )
            for u in range(UNROLL):
                slot = codes[section, block * UNROLL + u] >> 24
                out[slot] += products[u]
            return carry

        return lax.fori_loop(0, blocks, one_block, carry)

    lax.fori_loop(0, tasks, one_task, 0)


def add_terms(codes, meta, left, right, running, stage, slots, side):
    sections, allowed = tuple(stage), tuple(stage.values())
    tiles = tuple(sorted({t for some in allowed for t in some}))
    tasks = len(sections)
    operands = []

    def place(value):
        for k, known in enumerate(operands):
            if known is value:
                return k
        operands.append(value)
        return len(operands) - 1

    left_of = tuple(tuple((place(v), v.shape[0]) for v in left[s]) for s in sections)
    right_of = tuple(tuple((f, place(u), place(v), u.shape[0]) for f, u, v in right[t]) for t in tiles)
    if running is not None:
        operands.append(running)
    work = tasks * 96 * 2 * side * side * 2 * side
    return pl.pallas_call(
        functools.partial(product_kernel, (sections, allowed, tiles, left_of, right_of, running is not None)),
        out_shape=jax.ShapeDtypeStruct((slots, side, side), jnp.float32),
        in_specs=[pl.BlockSpec(memory_space=pltpu.SMEM)] * 2 + [pl.BlockSpec(memory_space=pl.ANY)] * len(operands),
        out_specs=pl.BlockSpec(memory_space=pltpu.VMEM),
        scratch_shapes=[
            pltpu.VMEM((tasks, slots + 1, side, side), jnp.bfloat16),
            pltpu.VMEM((tasks, slots, side, side), jnp.bfloat16),
            pltpu.SemaphoreType.DMA((tasks + 1, 2, 2)),
        ],
        compiler_params=pltpu.CompilerParams(vmem_limit_bytes=12 * 2**20),
        cost_estimate=pl.CostEstimate(flops=int(0.25 * work), bytes_accessed=4 * 2**20, transcendentals=0),
    )(codes, meta, *operands)


def body(x_blocks, x_live, pair_slots, pair_count):
    row_total = lax.axis_size("row")
    col_total = lax.axis_size("col")
    layers = row_total // col_total
    panel = lax.axis_index("row") // layers
    col = lax.axis_index("col")
    slots, side = x_blocks.shape[2], x_blocks.shape[3]
    half = slots // 2

    def place(p, w, z):
        return (p * layers + w) * col_total + z

    everyone = [(p, w, z) for p in range(col_total) for w in range(layers) for z in range(col_total)]

    def moved(value, source_of):
        pairs = []
        for p, w, z in everyone:
            q, y = source_of(p, z)
            pairs.append((place(q, w, y), place(p, w, z)))
        return lax.ppermute(value, AXES, pairs)

    filtered = jnp.where(x_live[0, 0][:, None, None] != 0, x_blocks[0, 0], jnp.zeros((), x_blocks.dtype))
    codes, entries = pair_codes(pair_slots[0, 0], pair_count[0, 0], slots)

    if col_total != SECTIONS:
        left, right = [], []
        for s in range(SECTIONS):
            left.append([filtered if s == 0 else moved(filtered, lambda p, z: (p, (z + s) % col_total))])
            value = moved(filtered, lambda p, z: (z, (p + s) % col_total))
            right.append([(0, value, value)])
        meta = jnp.concatenate([entries, jnp.zeros((4,), jnp.int32)])
        everything = {s: tuple(range(SECTIONS)) for s in range(SECTIONS)}
        total = add_terms(codes, meta, left, right, None, everything, slots, side)
        return total[None, None]

    near_x = panel % 2 == col % 2
    near_y = panel // 2 == col // 2
    next_y = panel // 2 == (col + 1) % SECTIONS // 2
    shift = (col - panel) % SECTIONS
    meta = jnp.concatenate([entries, jnp.stack([shift, near_x.astype(jnp.int32), near_y.astype(jnp.int32), 0 * shift])])
    made = {"a0": filtered[:half], "b0": filtered[half:]}
    ops = {}

    def op(name, operand, source_of):
        ops[name] = (operand, source_of)

    def get(name):
        if name not in made:
            if name in ops:
                operand, source_of = ops[name]
                value = operand()
                waits = [get(w) for w in AFTER.get(name, ())]
                if waits:
                    value = lax.optimization_barrier((value, *waits))[0]
                made[name] = moved(value, source_of)
            else:
                made[name] = values[name]()
        return made[name]

    def x_hop(p, z):
        return p ^ 1, z

    def y_hop(p, z):
        return p ^ 2, z

    def next_col(p, z):
        return p, (z + 1) % SECTIONS

    def last_col(p, z):
        return p, (z - 1) % SECTIONS

    values = {}
    for t in range(SECTIONS):
        la, lb = ("a0", "b0") if t == 0 else (f"L{t}A", f"L{t}B")
        if t:
            pa, pb = ("a0", "b0") if t == 1 else (f"L{t - 1}A", f"L{t - 1}B")
            op(la, functools.partial(get, pa), next_col)
            op(lb, functools.partial(get, pb), next_col)
        if t < SECTIONS - 1:
            op(f"X{t}A", functools.partial(get, la), x_hop)
            values[f"S{t}A"] = lambda t=t, la=la: lax.select(near_x, get(la), get(f"X{t}A"))
            op(f"Y{t}A", functools.partial(get, f"S{t}A"), y_hop)
            op(f"Y{t}B", functools.partial(get, lb), y_hop)
            values[f"S{t}B"] = lambda t=t, lb=lb: lax.select(near_y, get(lb), get(f"Y{t}B"))
            op(f"X{t}B", functools.partial(get, f"S{t}B"), x_hop)
    values["S0C"] = lambda: lax.select(near_x, get("X0A"), get("a0"))
    values["S0D"] = lambda: lax.select(next_y, get("b0"), get("Y0B"))
    op("Y0C", functools.partial(get, "S0C"), y_hop)
    op("X0D", functools.partial(get, "S0D"), x_hop)
    values["F0C"] = lambda: lax.select(next_y, get("S0C"), get("Y0C"))
    values["F0D"] = lambda: lax.select(near_x, get("X0D"), get("S0D"))
    op("R3A", functools.partial(get, "F0C"), last_col)
    op("R3B", functools.partial(get, "F0D"), last_col)

    def left_of(s):
        return [get("a0"), get("b0")] if s == 0 else [get(f"L{s}A"), get(f"L{s}B")]

    def right_of(t):
        if t == SECTIONS - 1:
            return [(0, get("R3A"), get("R3A")), (0, get("R3B"), get("R3B"))]
        return [(1, get(f"S{t}A"), get(f"Y{t}A")), (0, get(f"S{t}B"), get(f"X{t}B"))]

    def kernel_stage(k):
        stage = STAGES[k]
        tiles = sorted({t for some in stage.values() for t in some})
        left, right = {s: left_of(s) for s in stage}, {t: right_of(t) for t in tiles}
        running = get(f"K{k - 1}") if k else None
        return add_terms(codes, meta, left, right, running, stage, slots, side)

    for k in range(len(STAGES)):
        values[f"K{k}"] = functools.partial(kernel_stage, k)
    return get(f"K{len(STAGES) - 1}")[None, None]


def solution(mesh):
    return jax.shard_map(
        body,
        mesh=mesh,
        in_specs=(
            P("row", "col", None, None, None),
            P("row", "col", None),
            P("row", "col", None, None, None),
            P("row", "col", None),
        ),
        out_specs=P("row", "col", None, None, None),
        check_vma=False,
    )
```

```python
import functools

import jax
import jax.numpy as jnp
from jax import lax
from jax.experimental import pallas as pl
from jax.experimental.pallas import tpu as pltpu
from jax.sharding import PartitionSpec as P

SECTIONS = 4
UNROLL = 26
AXES = ("row", "col")
ROWS_BY_ROWS = (((1,), (1,)), ((), ()))
VLIM = 12
KSPACE = pl.ANY
AHEAD = 'AB'
FIRST = 8
COST = 0.25
KS = ({0: (0, 1), 1: (0, 1), 2: (0, 1)}, {0: (2, 3), 1: (2, 3), 2: (2, 3)}, {3: (0, 1, 2, 3)})
AFTER = {'L2B': ('Y0C',), 'L3A': ('R3B',), 'L3B': ('R3A',), 'X2A': ('X1A', 'Y1B'), 'X2B': ('X1A', 'X1B', 'Y1A', 'Y1B'), 'Y0C': ('X0A',), 'Y2A': ('X1A', 'Y1A', 'Y1B'), 'Y2B': ('X1A', 'Y1B')}


def pair_codes(pair_slots, pair_count, slots):
    pairs = pair_slots.shape[2]
    place = lax.iota(jnp.int32, pairs)
    left, right, out = pair_slots[:, 0], pair_slots[:, 1], pair_slots[:, 2]
    live = place[None, :] < pair_count[:, None]
    same = (out[:, :, None] == out[:, None, :]) & live[:, :, None] & live[:, None, :]
    rank = jnp.sum((same & (place[None, :] < place[:, None])[None]).astype(jnp.int32), axis=2)
    slot_ids = lax.iota(jnp.int32, slots)
    held = jnp.sum(((out[:, :, None] == slot_ids) & live[:, :, None]).astype(jnp.int32), axis=1)
    entries = (held + 1) // 2
    before = (out[:, :, None] > slot_ids).astype(jnp.int32)
    entry = jnp.sum(before * entries[:, None, :], axis=2) + rank // 2
    first = rank % 2 == 0
    part = jnp.where(first, (left - slots) + right * 2**12 + out * 2**24, (left - slots) * 2**6 + right * 2**18)
    room = (pairs + slots) // 2
    room = (room + UNROLL - 1) // UNROLL * UNROLL
    here = (entry[:, None, :] == lax.iota(jnp.int32, room)[None, :, None]) & live[:, None, :]
    codes = slots + slots * 2**6 + jnp.sum(jnp.where(here, part[:, None, :], 0), axis=2)
    return codes, jnp.sum(entries, axis=1)


def product_kernel(cfg, codes, meta, *refs):
    sections, allowed, tiles, left_of, right_of, has_sum = cfg
    tasks = len(sections)
    sum_ref = refs[-5] if has_sum else None
    out, left_buf, right_buf, sems = refs[-4:]
    slots = out.shape[0]
    shift = meta[SECTIONS]

    def tile_of(section):
        return lax.rem(section + SECTIONS - shift, SECTIONS)

    def wanted(i):
        tile = tile_of(sections[0] + i)
        yes = [tile == t for t in allowed[0]]
        if len(set(allowed)) > 1:
            yes = [(i == k) & (tile == t) for k in range(tasks) for t in allowed[k]]
        return functools.reduce(lambda a, b: a | b, yes)

    def copies(i):
        tile = tile_of(sections[i])
        wants = wanted(i)
        found = []
        start = 0
        for piece, (ref, size) in enumerate(left_of[i]):
            to = left_buf.at[i, pl.ds(start, size)]
            found.append((wants, pltpu.make_async_copy(refs[ref], to, sems.at[i, 0, piece])))
            start += size
        for t, pieces in zip(tiles, right_of):
            if t not in allowed[i]:
                continue
            start = 0
            for piece, (flag, near, far, size) in enumerate(pieces):
                to = right_buf.at[i, pl.ds(start, size)]
                sem = sems.at[i, 1, piece]
                if near == far:
                    found.append((tile == t, pltpu.make_async_copy(refs[near], to, sem)))
                else:
                    held = meta[SECTIONS + 1 + flag] == 1
                    found.append(((tile == t) & held, pltpu.make_async_copy(refs[near], to, sem)))
                    found.append(((tile == t) & ~held, pltpu.make_async_copy(refs[far], to, sem)))
                start += size
        return found

    for i in range(tasks):
        for condition, copy in copies(i):
            pl.when(condition)(copy.start)
    if has_sum:
        sum_copy = pltpu.make_async_copy(sum_ref, out, sems.at[tasks, 0, 0])
        sum_copy.start()
    for i in range(tasks):
        left_buf[i, slots] = jnp.zeros(left_buf.shape[2:], left_buf.dtype)
    if not has_sum:
        out[...] = jnp.zeros_like(out)

    def arrived(i):
        for side, (buf, sizes) in enumerate(
            ((left_buf, [n for _, n in left_of[0]]), (right_buf, [n for *_, n in right_of[0]]))
        ):
            start = 0
            for piece, size in enumerate(sizes):
                there = buf.at[i, pl.ds(start, size)]
                pltpu.make_async_copy(there, there, sems.at[i, side, piece]).wait()
                start += size

    if has_sum:
        sum_copy.wait()

    def one_task(i, carry):
        section = sections[0] + i
        pl.when(wanted(i))(lambda: arrived(i))
        blocks = jnp.where(wanted(i), (meta[section] + UNROLL - 1) // UNROLL, 0)

        def one_block(block, carry):
            products = []
            for u in range(UNROLL):
                code = codes[section, block * UNROLL + u]
                left = [left_buf[i, (code >> k) & 63] for k in (0, 6)]
                right = [right_buf[i, (code >> k) & 63] for k in (12, 18)]
                products.append(
                    lax.dot_general(
                        jnp.concatenate(left, axis=1),
                        jnp.concatenate(right, axis=1),
                        ROWS_BY_ROWS,
                        preferred_element_type=jnp.float32,
                    )
                )
            for u in range(UNROLL):
                slot = codes[section, block * UNROLL + u] >> 24
                out[slot] += products[u]
            return carry

        return lax.fori_loop(0, blocks, one_block, carry)

    lax.fori_loop(0, tasks, one_task, 0)


def add_terms(codes, meta, left, right, running, stage, slots, side):
    sections, allowed = tuple(stage), tuple(stage.values())
    tiles = tuple(sorted({t for some in allowed for t in some}))
    tasks = len(sections)
    operands = []

    def place(value):
        for k, known in enumerate(operands):
            if known is value:
                return k
        operands.append(value)
        return len(operands) - 1

    left_of = tuple(tuple((place(v), v.shape[0]) for v in left[s]) for s in sections)
    right_of = tuple(tuple((f, place(u), place(v), u.shape[0]) for f, u, v in right[t]) for t in tiles)
    if running is not None:
        operands.append(running)
    work = tasks * 96 * 2 * side * side * 2 * side
    return pl.pallas_call(
        functools.partial(product_kernel, (sections, allowed, tiles, left_of, right_of, running is not None)),
        out_shape=jax.ShapeDtypeStruct((slots, side, side), jnp.float32),
        in_specs=[pl.BlockSpec(memory_space=pltpu.SMEM)] * 2 + [pl.BlockSpec(memory_space=KSPACE)] * len(operands),
        out_specs=pl.BlockSpec(memory_space=pltpu.VMEM),
        scratch_shapes=[
            pltpu.VMEM((tasks, slots + 1, side, side), jnp.bfloat16),
            pltpu.VMEM((tasks, slots, side, side), jnp.bfloat16),
            pltpu.SemaphoreType.DMA((tasks + 1, 2, 2)),
        ],
        compiler_params=pltpu.CompilerParams(vmem_limit_bytes=VLIM * 2**20),
        cost_estimate=pl.CostEstimate(flops=int(COST * work), bytes_accessed=4 * 2**20, transcendentals=0),
    )(codes, meta, *operands)


def live_kernel(x_live, x_blocks, *refs):
    outs, (live, sems) = refs[:-2], refs[-2:]
    copies = [pltpu.make_async_copy(x_live, live, sems.at[len(outs)])]
    start = 0
    for k, out in enumerate(outs):
        copies.append(pltpu.make_async_copy(x_blocks.at[0, 0, pl.ds(start, out.shape[0])], out, sems.at[k]))
        start += out.shape[0]
    for copy in copies:
        copy.start()
    for copy in copies:
        copy.wait()
    start = 0
    for out in outs:
        for slot in range(out.shape[0]):

            @pl.when(live[0, 0, start + slot] == 0)
            def _(out=out, slot=slot):
                out[slot] = jnp.zeros(out.shape[1:], out.dtype)

        start += out.shape[0]


def keep_live(x_blocks, x_live, sizes):
    return pl.pallas_call(
        live_kernel,
        out_shape=[jax.ShapeDtypeStruct((n, *x_blocks.shape[3:]), x_blocks.dtype) for n in sizes],
        in_specs=[pl.BlockSpec(memory_space=pl.ANY)] * 2,
        out_specs=[pl.BlockSpec(memory_space=pltpu.VMEM)] * len(sizes),
        scratch_shapes=[
            pltpu.SMEM(x_live.shape, x_live.dtype),
            pltpu.SemaphoreType.DMA((len(sizes) + 1,)),
        ],
        compiler_params=pltpu.CompilerParams(vmem_limit_bytes=60 * 2**20),
        cost_estimate=pl.CostEstimate(flops=0, bytes_accessed=2**20, transcendentals=0),
    )(x_live, x_blocks)


def body(x_blocks, x_live, pair_slots, pair_count):
    row_total = lax.axis_size("row")
    col_total = lax.axis_size("col")
    layers = row_total // col_total
    panel = lax.axis_index("row") // layers
    col = lax.axis_index("col")
    slots, side = x_blocks.shape[2], x_blocks.shape[3]
    half = slots // 2

    def place(p, w, z):
        return (p * layers + w) * col_total + z

    everyone = [(p, w, z) for p in range(col_total) for w in range(layers) for z in range(col_total)]

    def moved(value, source_of):
        pairs = []
        for p, w, z in everyone:
            if source_of(p, z) is not None:
                q, y = source_of(p, z)
                pairs.append((place(q, w, y), place(p, w, z)))
        return lax.ppermute(value, AXES, pairs)

    codes, entries = pair_codes(pair_slots[0, 0], pair_count[0, 0], slots)

    if col_total != SECTIONS:
        (filtered,) = keep_live(x_blocks, x_live, (slots,))
        left, right = [], []
        for s in range(SECTIONS):
            left.append([filtered if s == 0 else moved(filtered, lambda p, z: (p, (z + s) % col_total))])
            value = moved(filtered, lambda p, z: (z, (p + s) % col_total))
            right.append([(0, value, value)])
        meta = jnp.concatenate([entries, jnp.zeros((4,), jnp.int32)])
        everything = {s: tuple(range(SECTIONS)) for s in range(SECTIONS)}
        total = add_terms(codes, meta, left, right, None, everything, slots, side)
        return total[None, None]

    near_x = panel % 2 == col % 2
    near_y = panel // 2 == col // 2
    next_y = panel // 2 == (col + 1) % SECTIONS // 2
    shift = (col - panel) % SECTIONS
    meta = jnp.concatenate([entries, jnp.stack([shift, near_x.astype(jnp.int32), near_y.astype(jnp.int32), 0 * shift])])
    done = {}

    def hop(name, value, source_of):
        waits = AFTER.get(name, ())
        if waits:
            value = lax.optimization_barrier((value,) + tuple(done[n] for n in waits))[0]
        with jax.named_scope(name):
            done[name] = moved(value, source_of)
        return done[name]

    def in_plane(name, value, flip, offset, far=False):
        def source_of(p, z):
            q = (z + offset) % SECTIONS
            return (p ^ flip, z) if p ^ flip == q or (far and p ^ flip == q ^ (3 - flip)) else None

        return hop(name, value, source_of)

    def along(name, value, by):
        return hop(name, value, lambda p, z: (p, (z + by) % SECTIONS))

    near = {1: near_x, 2: near_y}

    def stage_kernel(name, before, stage):
        done[name] = add_terms(codes, meta, left, right, done.get(before), stage, slots, side)

    made = dict(zip(("a0", "b0"), keep_live(x_blocks, x_live, (FIRST, slots - FIRST))))
    ops = {}

    def op(name, operand, source_of):
        ops[name] = (operand, source_of)

    def get(name):
        if name not in made:
            if name in ops:
                operand, source_of = ops[name]
                value = operand()
                waits = [get(w) for w in AFTER.get(name, ())]
                if waits:
                    value = lax.optimization_barrier((value, *waits))[0]
                with jax.named_scope(name):
                    made[name] = moved(value, source_of)
            else:
                made[name] = values[name]()
        return made[name]

    def x_hop(p, z):
        return p ^ 1, z

    def y_hop(p, z):
        return p ^ 2, z

    def next_col(p, z):
        return p, (z + 1) % SECTIONS

    def last_col(p, z):
        return p, (z - 1) % SECTIONS

    values = {}
    for t in range(SECTIONS):
        la, lb = ("a0", "b0") if t == 0 else (f"L{t}A", f"L{t}B")
        if t:
            pa, pb = ("a0", "b0") if t == 1 else (f"L{t - 1}A", f"L{t - 1}B")
            op(la, functools.partial(get, pa), next_col)
            op(lb, functools.partial(get, pb), next_col)
        if t < SECTIONS - 1 or "A" not in AHEAD:
            op(f"X{t}A", functools.partial(get, la), x_hop)
            values[f"S{t}A"] = lambda t=t, la=la: lax.select(near_x, get(la), get(f"X{t}A"))
            op(f"Y{t}A", functools.partial(get, f"S{t}A"), y_hop)
        if t < SECTIONS - 1 or "B" not in AHEAD:
            op(f"Y{t}B", functools.partial(get, lb), y_hop)
            values[f"S{t}B"] = lambda t=t, lb=lb: lax.select(near_y, get(lb), get(f"Y{t}B"))
            op(f"X{t}B", functools.partial(get, f"S{t}B"), x_hop)
    if AHEAD:
        values["S0C"] = lambda: lax.select(near_x, get("X0A"), get("a0"))
        values["S0D"] = lambda: lax.select(next_y, get("b0"), get("Y0B"))
        op("Y0C", functools.partial(get, "S0C"), y_hop)
        op("X0D", functools.partial(get, "S0D"), x_hop)
        values["F0C"] = lambda: lax.select(next_y, get("S0C"), get("Y0C"))
        values["F0D"] = lambda: lax.select(near_x, get("X0D"), get("S0D"))
        op("R3A", functools.partial(get, "F0C"), last_col)
        op("R3B", functools.partial(get, "F0D"), last_col)

    def left_of(s):
        return [get("a0"), get("b0")] if s == 0 else [get(f"L{s}A"), get(f"L{s}B")]

    def right_of(t):
        ahead = AHEAD if t == SECTIONS - 1 else ""
        a = (0, get("R3A"), get("R3A")) if "A" in ahead else (1, get(f"S{t}A"), get(f"Y{t}A"))
        b = (0, get("R3B"), get("R3B")) if "B" in ahead else (0, get(f"S{t}B"), get(f"X{t}B"))
        return [a, b]

    def kernel_stage(k):
        stage = KS[k]
        tiles = sorted({t for some in stage.values() for t in some})
        left, right = {s: left_of(s) for s in stage}, {t: right_of(t) for t in tiles}
        running = get(f"K{k - 1}") if k else None
        waits = [get(w) for w in AFTER.get(f"K{k}", ())]
        c = codes
        if waits:
            c = lax.optimization_barrier((codes, *waits))[0]
        return add_terms(c, meta, left, right, running, stage, slots, side)

    for k in range(len(KS)):
        values[f"K{k}"] = functools.partial(kernel_stage, k)
    done["K3"] = get(f"K{len(KS) - 1}")
    return done["K3"][None, None]


def solution(mesh):
    return jax.shard_map(
        body,
        mesh=mesh,
        in_specs=(
            P("row", "col", None, None, None),
            P("row", "col", None),
            P("row", "col", None, None, None),
            P("row", "col", None),
        ),
        out_specs=P("row", "col", None, None, None),
        check_vma=False,
    )
```
